32 devices in a mesh: seq: 4 (over x, core), head: 8 (over z, y).
Axes of the slice: x: 2, y: 2, z: 4, core: 2. Of those that a mesh axis runs over, the one named last changes fastest.
Arguments:
- queries: bfloat16 [512, 8192], P('seq', 'head'), may hold values from -256 to 256
- key_rows: bfloat16 [512, 128], P('seq'), may hold values from -6 to 6
- value_rows: bfloat16 [512, 128], P('seq'), may hold values from -6 to 6
- pair_keys: bfloat16 [512, 128], P('seq'), may hold values from 0.27 to 1.73
- pair_values: bfloat16 [512, 128], P('seq'), may hold values from 0.099609375 to 1.8984375
- first_key: int32 [512], P('seq'), may hold values from 0 to 511, as said below
- residual: float32 [512, 8192], P(('seq', 'head')), may hold values from -6 to 6
- out_weight: bfloat16 [8192, 8192], P('head', 'seq'), may hold values from -0.25 to 0.25
Outputs:
- updated: float32 [512, 8192], P(('seq', 'head'))
The draws below stay inside these ranges and needn't reach their ends.
Inputs may be any that keep to these rules, and one draw needn't show every extreme that they name: first_key never falls along the tokens, first_key[i] <= i, and first_key[i] = i where a document begins; positions 0 and 511 begin one.
All inputs are finite; a program needn't handle non-finite values.
Results may differ from the reference program's by a relative error of at most 0.005.
Values may be sent and summed in bfloat16 or wider, within the bound.
No kernel may reach another device: no remote copies, remote signals or barrier semaphores. Data moves between devices by JAX's collectives and lax.ppermute only.
A program may use at most 128 MiB of HBM per device.

```python
import math
import jax
import jax.numpy as jnp
from jax import lax

D = 8192
HEADS = 64
DH = 128
W1 = 512
W2 = 32
TOKENS = 512


def drawn_draw(key):
    base_key = jax.random.fold_in(key, 5)
    key_first, key_second, key_third = jax.random.split(base_key, 3)
    key_table = jnp.clip(jax.random.normal(key_first, (TOKENS, DH), jnp.float32), -6.0, 6.0)
    pair_table = 1.0 + 0.18 * jnp.clip(jax.random.normal(key_second, (TOKENS, DH), jnp.float32), -4.0, 4.0)
    query_table = jnp.clip(jax.random.normal(key_third, (TOKENS, HEADS, DH), jnp.float32), -6.0, 6.0)
    return (query_table.reshape(TOKENS, HEADS * DH), key_table, pair_table)


def draw_queries(key, part):
    return drawn_draw(key)[0].astype(jnp.bfloat16)


def draw_key_rows(key, part):
    return drawn_draw(key)[1].astype(jnp.bfloat16)


def draw_pair_keys(key, part):
    return drawn_draw(key)[2].astype(jnp.bfloat16)


def draw_first_key(key, part):
    count_starts = max(2, TOKENS // 256)
    start_rows = jax.random.randint(jax.random.fold_in(key, 11), (count_starts,), 1, TOKENS)
    flags = jnp.zeros((TOKENS,), jnp.int32).at[start_rows].set(1).at[0].set(1).at[TOKENS - 1].set(1)
    positions = jnp.arange(TOKENS, dtype=jnp.int32)
    return lax.cummax(jnp.where(flags > 0, positions, 0), axis=0)


def level_of(key, extent, cuts, least, high):
    def one(axis_at, parts):
        heights = jax.random.uniform(jax.random.fold_in(jax.random.fold_in(key, 6), axis_at), (parts,), jnp.float32, least / len(cuts), high / len(cuts))
        return jnp.repeat(jnp.exp(heights), extent[axis_at] // parts).reshape((-1,) + (1,) * (len(extent) - axis_at - 1))

    factor_of = one(*cuts[0])
    for cut in cuts[1:]:
        factor_of = factor_of * one(*cut)
    return factor_of


def normal_values(stream_key, extent, deviation, bound, shards=(), kind=jnp.bfloat16):
    result = jax.random.normal(stream_key, extent, jnp.float32) * deviation
    if len(shards) > 0:
        result = level_of(stream_key, extent, shards, -0.22, 0.18) * result
    return jnp.clip(result, min=-bound, max=bound).astype(kind)


def setup_inputs(seed: int = 0) -> dict:
    arg_keys = jax.random.split(jax.random.key(seed), 9)
    return {
        "queries": draw_queries(jax.random.fold_in(arg_keys[8], 71), 0),
        "key_rows": draw_key_rows(jax.random.fold_in(arg_keys[8], 71), 0),
        "value_rows": normal_values(arg_keys[2], (TOKENS, DH), 1.0, 6.0, ((0, 4),)),
        "pair_keys": draw_pair_keys(jax.random.fold_in(arg_keys[8], 71), 0),
        "pair_values": jnp.clip(1.0 + 0.18 * jax.random.normal(arg_keys[4], (TOKENS, DH), jnp.float32), 0.099609375, 1.8984375).astype(jnp.bfloat16),
        "first_key": draw_first_key(jax.random.fold_in(arg_keys[8], 71), 0),
        "residual": normal_values(arg_keys[6], (TOKENS, D), 1.0, 6.0, ((0, 32),), jnp.float32),
        "out_weight": normal_values(arg_keys[7], (HEADS * DH, D), (HEADS * DH // 16) ** -0.5, 0.25, ((0, 8), (1, 4))),
    }


MASKED_SCORE = -1e+30

def reference(queries, key_rows, value_rows, pair_keys, pair_values, first_key, residual, out_weight):
    scale_factor = 1.0 / math.sqrt(DH)
    qblock = 16
    key_padded = jnp.concatenate([jnp.zeros((W1, DH), key_rows.dtype), key_rows], axis=0)
    value_padded = jnp.concatenate([jnp.zeros((W1, DH), value_rows.dtype), value_rows], axis=0)
    pair_key_padded = jnp.concatenate([jnp.zeros((W2, DH), pair_keys.dtype), pair_keys], axis=0)
    pair_value_padded = jnp.concatenate([jnp.zeros((W2, DH), pair_values.dtype), pair_values], axis=0)
    unfold_index = (jnp.arange(TOKENS, dtype=jnp.int32)[:, None] + 1 + jnp.arange(W2, dtype=jnp.int32)[None, :]).astype(jnp.int32)
    pair_key_win = pair_key_padded[unfold_index]
    pair_value_win = pair_value_padded[unfold_index]
    query_heads = queries.reshape(TOKENS, HEADS, DH)

    def attend(row_start):
        query_blk = lax.dynamic_slice_in_dim(query_heads, row_start, qblock, 0).astype(jnp.float32)
        pair_kblk = lax.dynamic_slice_in_dim(pair_key_win, row_start, qblock, 0).astype(jnp.float32)
        pair_vblk = lax.dynamic_slice_in_dim(pair_value_win, row_start, qblock, 0).astype(jnp.float32)
        pair_mix = (query_blk[:, :, None, :] * pair_kblk[:, None, :, :]).astype(jnp.bfloat16)
        key_blk = lax.dynamic_slice_in_dim(key_padded, row_start, W1 + qblock, 0).astype(jnp.float32)
        value_blk = lax.dynamic_slice_in_dim(value_padded, row_start, W1 + qblock, 0).astype(jnp.float32)
        logits = jnp.einsum('ahod,kd->ahok', pair_mix.astype(jnp.float32), key_blk) * scale_factor
        query_pos = row_start + jnp.arange(qblock, dtype=jnp.int32)
        key_pos = row_start - W1 + jnp.arange(W1 + qblock, dtype=jnp.int32)
        pair_pos = query_pos[:, None] - W2 + 1 + jnp.arange(W2, dtype=jnp.int32)[None, :]
        lower_bound = lax.dynamic_slice_in_dim(first_key, row_start, qblock, 0)
        key_ok = (key_pos[None, :] <= query_pos[:, None]) & (key_pos[None, :] > query_pos[:, None] - W1) & (key_pos[None, :] >= lower_bound[:, None])
        pair_ok = pair_pos >= lower_bound[:, None]
        allowed = key_ok[:, None, None, :] & pair_ok[:, None, :, None]
        logits = jnp.where(allowed, logits, MASKED_SCORE)
        row_top = lax.optimization_barrier(jnp.max(logits, axis=(2, 3), keepdims=True))
        expo = jnp.where(allowed, jnp.exp(logits - row_top), 0.0)
        row_total = lax.optimization_barrier(jnp.sum(expo, axis=(2, 3), keepdims=True))
        rounded_weight = (expo / row_total).astype(jnp.bfloat16)
        carried = jnp.einsum('ahok,kd->ahod', rounded_weight.astype(jnp.float32), value_blk)
        return lax.optimization_barrier(jnp.sum(carried * pair_vblk[:, None, :, :], axis=2)).astype(jnp.bfloat16)
    starts = jnp.arange(TOKENS // qblock, dtype=jnp.int32) * qblock
    attended = lax.map(attend, starts).reshape(TOKENS, HEADS * DH)
    return residual + jnp.dot(attended, out_weight, preferred_element_type=jnp.float32)
```

```python
import math, functools
import jax, jax.numpy as jnp
from jax import lax
from jax.experimental import pallas as pl
from jax.experimental.pallas import tpu as pltpu
from jax.sharding import PartitionSpec as P
DH=128; W1=512; W2=32
G=4
BK=128
LOW=-1e30

def attn_kernel(own_row, max_blocks, base_ref, fk_ref, q_ref, ctx_ref, out_ref, pkf, pk2, pvb, kx, vx, lhs, s_ref, p_ref):
    tok = fk_ref.shape[0]
    seq_base = base_ref[0]
    ctx_base = base_ref[1]
    own = pl.multiple_of(seq_base - ctx_base, 128)
    rim = pl.multiple_of(jnp.maximum(own - W2, 0), W2)
    kx[:, :DH] = ctx_ref[:, :DH]
    vx[:, :DH] = ctx_ref[:, DH:2*DH]
    vx[:, DH:] = jnp.ones_like(vx[:, DH:])
    pkf[0:W2] = ctx_ref[pl.ds(rim, W2), 2*DH:].astype(jnp.float32)
    pkf[W2:W2+tok] = ctx_ref[pl.ds(own, tok), 2*DH:].astype(jnp.float32)
    pkf[W2+tok:] = jnp.zeros_like(pkf[W2+tok:])
    rows = W2 + tok
    def spread(blk, _):
        r0 = pl.multiple_of(blk*8, 8)
        x = pkf[pl.ds(r0, 16)]
        for r in range(8):
            a = jnp.broadcast_to(x[r:r+1, :DH], (8, DH))
            b = jnp.broadcast_to(x[r+1:r+2, :DH], (8, DH))
            pk2[r0 + r] = jnp.concatenate([a, b], axis=0).astype(jnp.bfloat16)
            pvb[r0 + r] = jnp.broadcast_to(x[r:r+1, DH:], (8, DH))
        return 0
    lax.fori_loop(0, rows//8, spread, 0)
    row = lax.broadcasted_iota(jnp.int32, (G*256, DH), 0)
    col = lax.broadcasted_iota(jnp.int32, (G*256, DH), 1)
    lhs[:, DH:] = jnp.where(row // 8 == col, 1.0, 0.0).astype(jnp.bfloat16)
    lane = lax.broadcasted_iota(jnp.int32, (1, DH), 1)
    lane_t = lane // W2
    lane_o = lane % W2
    c2 = math.log2(math.e)/math.sqrt(DH)

    def group(g, _):
        i0 = g*G
        pos0 = seq_base + i0
        first = [fk_ref[i0+t] for t in range(G)]
        lo_pos = jnp.maximum(first[0], pos0 - W1 + 1)
        kb_lo = (lo_pos - ctx_base)//BK
        kb_hi = (pos0 + G - 1 - ctx_base)//BK
        nb = kb_hi - kb_lo + 1
        start = pl.multiple_of(kb_lo*BK, BK)
        for t in range(G):
            q = q_ref[pl.ds(pl.multiple_of((i0+t)*16, 16), 16)]
            for k in range(W2//2):
                lhs[t*256+k*16:t*256+(k+1)*16, :DH] = q*pk2[i0+t+1+2*k]
        fk_lane = jnp.full((1, DH), first[G-1], jnp.int32)
        for t in range(G-2, -1, -1):
            fk_lane = jnp.where(lane_t == t, first[t], fk_lane)
        pos_lane = pos0 + lane_t
        low_lane = jnp.maximum(fk_lane, pos_lane - W1 + 1)
        low_lane = jnp.where(pos_lane - (W2-1) + lane_o >= fk_lane, low_lane, 2**30)

        def run(n):
            keys = n*BK
            jpos = lax.broadcasted_iota(jnp.int32, (keys, DH), 0) + (ctx_base + start)
            ok = (jpos >= low_lane) & (jpos <= pos_lane)
            kx[pl.ds(start, keys), DH:] = jnp.where(ok, 0.0, LOW).astype(jnp.bfloat16)
            s_ref[:, :keys] = lax.dot_general(lhs[...], kx[pl.ds(start, keys)], (((1,),(1,)),((),())), preferred_element_type=jnp.float32)
            for t in range(G):
                s = s_ref[t*256:(t+1)*256, :keys].reshape(W2, 8, keys)
                m = jnp.max(jnp.max(s, axis=0), axis=1, keepdims=True)
                p = jnp.exp2((s - m[None])*c2)
                p_ref[t*256:(t+1)*256, :keys] = p.reshape(256, keys).astype(jnp.bfloat16)
            o = jnp.dot(p_ref[:, :keys], vx[pl.ds(start, keys)], preferred_element_type=jnp.float32)
            outs = []
            for t in range(G):
                num = jnp.zeros((8, DH), jnp.float32)
                den = jnp.zeros((8, DH), jnp.float32)
                for w in range(W2):
                    r = t*256+w*8
                    num += o[r:r+8, :DH]*pvb[i0+t+1+w]
                    den += o[r:r+8, DH:]
                outs.append(num/den)
            out_ref[pl.ds(pl.multiple_of(i0*8, 32), G*8)] = jnp.concatenate(outs, axis=0).astype(jnp.bfloat16)
        for n in range(1, max_blocks+1):
            pl.when(nb == n)(functools.partial(run, n))
        return 0
    lax.fori_loop(0, tok//G, group, 0)

def attention(base, first_key, q2, ctx):
    tok = first_key.shape[0]
    rows = ctx.shape[0]
    mb = min(rows//BK, W1//BK+1)
    f32=jnp.float32; bf=jnp.bfloat16
    return pl.pallas_call(
        functools.partial(attn_kernel, None, mb),
        out_shape=jax.ShapeDtypeStruct((tok*8, DH), bf),
        in_specs=[pl.BlockSpec(memory_space=pltpu.SMEM)]*2+[pl.BlockSpec(memory_space=pltpu.VMEM)]*2,
        out_specs=pl.BlockSpec(memory_space=pltpu.VMEM),
        scratch_shapes=[
            pltpu.VMEM((W2+tok+8, 2*DH), f32),
            pltpu.VMEM((W2+tok, 16, DH), bf),
            pltpu.VMEM((W2+tok, 8, DH), f32),
            pltpu.VMEM((rows, 2*DH), bf),
            pltpu.VMEM((rows, 2*DH), bf),
            pltpu.VMEM((G*256, 2*DH), bf),
            pltpu.VMEM((G*256, mb*BK), f32),
            pltpu.VMEM((G*256, mb*BK), bf),
        ],
        compiler_params=pltpu.CompilerParams(vmem_limit_bytes=48*2**20),
        name="attention",
    )(base, first_key, q2, ctx)


def context_rows(block, reach):
    count = lax.axis_size("seq")
    tok = block.shape[0]
    if count <= reach + 1:
        return lax.all_gather(block, "seq", axis=0, tiled=True), lax.axis_index("seq") * tok
    pieces = [
        lax.ppermute(block, "seq", [(a, a + steps) for a in range(count - steps)])
        for steps in range(reach, 0, -1)
    ]
    return jnp.concatenate(pieces + [block], axis=0), reach * tok


def gathered(value):
    count = lax.axis_size("seq")
    if count & (count - 1):
        return lax.all_gather(value, "seq", axis=0)
    me = lax.axis_index("seq")
    value = value[None]
    bit = count // 2
    while bit:
        other = lax.ppermute(value, "seq", [(a, a ^ bit) for a in range(count)])
        high = (me & bit) > 0
        first = jnp.where(high, other, value)
        second = jnp.where(high, value, other)
        value = jnp.stack([first, second], axis=1).reshape((-1,) + value.shape[1:])
        bit //= 2
    return value


def local(queries, key_rows, value_rows, pair_keys, pair_values, first_key, residual, out_weight):
    tok = queries.shape[0]
    heads = queries.shape[1] // DH
    seq_size, head_size = lax.axis_size("seq"), lax.axis_size("head")
    block = jnp.concatenate([key_rows, value_rows, pair_keys, pair_values], axis=1)
    context, ahead = context_rows(block, (W1 + tok - 1) // tok)
    seq_base = lax.axis_index("seq") * tok
    base = jnp.stack([seq_base, seq_base - ahead]).astype(jnp.int32)
    q = queries.reshape(tok, heads, DH)
    slots = (heads + 7) // 8 * 8
    if slots > heads:
        q = jnp.concatenate([q, jnp.zeros((tok, slots - heads, DH), q.dtype)], axis=1)
    parts = []
    for at in range(0, slots, 8):
        tile = q[:, at : at + 8]
        both = jnp.concatenate([tile, tile], axis=1).reshape(tok * 16, DH)
        parts.append(attention(base, first_key, both, context).reshape(tok, 8, DH))
    features = (parts[0] if len(parts) == 1 else jnp.concatenate(parts, axis=1))[:, :heads]
    features = features.reshape(tok, heads * DH)
    every = gathered(features).reshape(seq_size * tok, heads * DH)
    partial_rows = jnp.dot(every, out_weight, preferred_element_type=jnp.float32)
    columns = out_weight.shape[1]
    rows = tok // head_size
    sent = partial_rows.astype(jnp.bfloat16).reshape(seq_size * head_size, rows, columns)
    got = lax.all_to_all(sent, ("seq", "head"), 0, 0).reshape(seq_size, head_size, rows, columns)
    summed = jnp.sum(got.astype(jnp.float32), axis=1)
    return residual + jnp.swapaxes(summed, 0, 1).reshape(rows, seq_size * columns)


def solution(mesh):
    placed = (
        P("seq", "head"),
        P("seq", None),
        P("seq", None),
        P("seq", None),
        P("seq", None),
        P("seq"),
        P(("seq", "head"), None),
        P("head", "seq"),
    )
    return jax.shard_map(
        local, mesh=mesh, in_specs=placed, out_specs=P(("seq", "head"), None), check_vma=False
    )
```

```python
import functools
import math

import jax
import jax.numpy as jnp
from jax import lax
from jax.experimental import pallas as pl
from jax.experimental.pallas import tpu as pltpu
from jax.sharding import PartitionSpec as P

DH = 128
W1 = 512
W2 = 32
BLOCK = 128
LOW = -1e30
TILE = 8
GROUP = 4
GROUPS = 2
ROWS = TILE * W2


def attention_kernel(
    first_token, count, most, stride, own_ref, base_ref, first_ref, q_ref, ctx_ref, pk_ref, pv_ref,
    out_ref, qf, of, pkf, pk2, pvb, kx, vx, lhs, scores, weights,
):
    blocks = kx.shape[1] // BLOCK
    tok = pk_ref.shape[0]
    own = own_ref[0]
    base = base_ref[0]
    origin = base - own * tok
    per = tok // BLOCK
    for b in range(blocks):
        at = b // per * stride + b % per * BLOCK
        rows = slice(b * BLOCK, (b + 1) * BLOCK)
        for g in range(GROUPS):
            kx[g, rows, :DH] = ctx_ref[at : at + BLOCK, :DH]
        vx[rows, :DH] = ctx_ref[at : at + BLOCK, DH:]
        vx[rows, DH:] = jnp.ones((BLOCK, DH), jnp.bfloat16)
    if first_token == 0:
        before = pl.multiple_of(jnp.maximum(own - 1, 0) * stride + tok, W2)
        pkf[0:W2] = ctx_ref[pl.ds(before, W2)].astype(jnp.float32)
    else:
        pkf[0:W2, :DH] = pk_ref[first_token - W2 : first_token].astype(jnp.float32)
        pkf[0:W2, DH:] = pv_ref[first_token - W2 : first_token].astype(jnp.float32)
    pkf[W2 : W2 + count, :DH] = pk_ref[first_token : first_token + count].astype(jnp.float32)
    pkf[W2 : W2 + count, DH:] = pv_ref[first_token : first_token + count].astype(jnp.float32)
    pkf[W2 + count :] = jnp.zeros((8, 2 * DH), jnp.float32)

    def spread(blk, _):
        r0 = pl.multiple_of(blk * 8, 8)
        x = pkf[pl.ds(r0, 16)]
        for r in range(8):
            a = jnp.broadcast_to(x[r : r + 1, :DH], (TILE, DH))
            b = jnp.broadcast_to(x[r + 1 : r + 2, :DH], (TILE, DH))
            pk2[r0 + r] = jnp.concatenate([a, b], axis=0).astype(jnp.bfloat16)
            pvb[r0 + r] = jnp.broadcast_to(x[r : r + 1, DH:], (TILE, DH))
        return 0

    lax.fori_loop(0, (W2 + count) // 8, spread, 0)
    for h in range(TILE):
        qf[pl.ds(h, count, stride=TILE), :] = q_ref[
            first_token : first_token + count, h * DH : (h + 1) * DH
        ].astype(jnp.float32)
    unit = GROUP * ROWS
    row = lax.broadcasted_iota(jnp.int32, (unit, DH), 0)
    col = lax.broadcasted_iota(jnp.int32, (unit, DH), 1)
    pick = jnp.where(row // TILE == col, 1.0, 0.0).astype(jnp.bfloat16)
    for g in range(GROUPS):
        lhs[g * unit : (g + 1) * unit, DH:] = pick
    lane = lax.broadcasted_iota(jnp.int32, (1, DH), 1)
    lane_token = lane // W2
    lane_offset = lane % W2
    factor = math.log2(math.e) / math.sqrt(DH)
    tokens = GROUP * GROUPS

    def step(index, _):
        i0 = index * tokens
        pos0 = base + first_token + i0
        first = [first_ref[first_token + i0 + t] for t in range(tokens)]
        lowest = jnp.maximum(first[0], pos0 - W1 + 1)
        block_low = (lowest - origin) // BLOCK
        block_high = (pos0 + tokens - 1 - origin) // BLOCK
        start = pl.multiple_of(block_low * BLOCK, BLOCK)

        def run(n):
            keys = n * BLOCK
            key_pos = lax.broadcasted_iota(jnp.int32, (keys, DH), 0) + (origin + start)

            def score(g):
                mine = first[g * GROUP : (g + 1) * GROUP]
                first_lane = jnp.full((1, DH), mine[-1], jnp.int32)
                for t in range(GROUP - 2, -1, -1):
                    first_lane = jnp.where(lane_token == t, mine[t], first_lane)
                high = pos0 + g * GROUP + lane_token
                low = jnp.maximum(first_lane, high - W1 + 1)
                low = jnp.where(high - (W2 - 1) + lane_offset >= first_lane, low, 2**30)
                ok = (key_pos >= low) & (key_pos <= high)
                kx[g, pl.ds(start, keys), DH:] = jnp.where(ok, 0.0, LOW).astype(jnp.bfloat16)
                for t in range(g * GROUP, (g + 1) * GROUP):
                    q = qf[pl.ds(pl.multiple_of((i0 + t) * TILE, TILE), TILE)]
                    q = jnp.concatenate([q, q], axis=0).astype(jnp.bfloat16)
                    for k in range(W2 // 2):
                        at = t * ROWS + k * 16
                        lhs[at : at + 16, :DH] = q * pk2[i0 + t + 1 + 2 * k]
                scores[g * unit : (g + 1) * unit, :keys] = lax.dot_general(
                    lhs[g * unit : (g + 1) * unit],
                    kx[g, pl.ds(start, keys)],
                    (((1,), (1,)), ((), ())),
                    preferred_element_type=jnp.float32,
                )

            def soften(g):
                for t in range(g * GROUP, (g + 1) * GROUP):
                    rows = slice(t * ROWS, (t + 1) * ROWS)
                    s = scores[rows, :keys].reshape(W2, TILE, keys)
                    top = jnp.max(jnp.max(s, axis=0), axis=1, keepdims=True)
                    e = jnp.exp2((s - top[None]) * factor)
                    weights[rows, :keys] = e.reshape(ROWS, keys).astype(jnp.bfloat16)

            def value(g):
                o = jnp.dot(
                    weights[g * unit : (g + 1) * unit, :keys],
                    vx[pl.ds(start, keys)],
                    preferred_element_type=jnp.float32,
                )
                for t in range(GROUP):
                    carried = jnp.zeros((TILE, DH), jnp.float32)
                    total = jnp.zeros((TILE, DH), jnp.float32)
                    for w in range(W2):
                        at = t * ROWS + w * TILE
                        carried += o[at : at + TILE, :DH] * pvb[i0 + g * GROUP + t + 1 + w]
                        total += o[at : at + TILE, DH:]
                    at = pl.multiple_of((i0 + g * GROUP + t) * TILE, TILE)
                    of[pl.ds(at, TILE)] = carried / total

            score(0)
            for g in range(GROUPS):
                if g + 1 < GROUPS:
                    score(g + 1)
                soften(g)
                if g >= 1:
                    value(g - 1)
            value(GROUPS - 1)

        for n in range(1, most + 1):
            pl.when(block_high - block_low + 1 == n)(functools.partial(run, n))
        return 0

    lax.fori_loop(0, count // tokens, step, 0)
    for h in range(TILE):
        out_ref[:, h * DH : (h + 1) * DH] = of[pl.ds(h, count, stride=TILE), :].astype(jnp.bfloat16)


def attention(first_token, count, own, base, first_key, q, context, pair_keys, pair_values):
    tok = pair_keys.shape[0]
    stride = tok + W2
    rows = context.shape[0] // stride * tok
    most = min(rows // BLOCK, W1 // BLOCK + 1)
    f32, bf16 = jnp.float32, jnp.bfloat16
    unit = GROUPS * GROUP * ROWS
    return pl.pallas_call(
        functools.partial(attention_kernel, first_token, count, most, stride),
        out_shape=jax.ShapeDtypeStruct((count, TILE * DH), bf16),
        in_specs=[pl.BlockSpec(memory_space=pltpu.SMEM)] * 3
        + [pl.BlockSpec(memory_space=pltpu.VMEM)] * 4,
        out_specs=pl.BlockSpec(memory_space=pltpu.VMEM),
        scratch_shapes=[
            pltpu.VMEM((count * TILE, DH), f32),
            pltpu.VMEM((count * TILE, DH), f32),
            pltpu.VMEM((W2 + count + 8, 2 * DH), f32),
            pltpu.VMEM((W2 + count, 2 * TILE, DH), bf16),
            pltpu.VMEM((W2 + count, TILE, DH), f32),
            pltpu.VMEM((GROUPS, rows, 2 * DH), bf16),
            pltpu.VMEM((rows, 2 * DH), bf16),
            pltpu.VMEM((unit, 2 * DH), bf16),
            pltpu.VMEM((unit, most * BLOCK), f32),
            pltpu.VMEM((unit, most * BLOCK), bf16),
        ],
        compiler_params=pltpu.CompilerParams(vmem_limit_bytes=40 * 2**20),
        name="attention",
    )(own, base, first_key, q, context, pair_keys, pair_values)


def context_blocks(block, reach):
    count = lax.axis_size("seq")
    if count <= reach + 1:
        return lax.all_gather(block, "seq", axis=0, tiled=True), lax.axis_index("seq")
    pieces = [
        lax.ppermute(block, "seq", [(a, a + steps) for a in range(count - steps)])
        for steps in range(reach, 0, -1)
    ]
    return jnp.concatenate(pieces + [block], axis=0), jnp.int32(reach)


def gathered(value):
    count = lax.axis_size("seq")
    if count & (count - 1):
        return lax.all_gather(value, "seq", axis=0)
    me = lax.axis_index("seq")
    value = value[None]
    bit = count // 2
    while bit:
        other = lax.ppermute(value, "seq", [(a, a ^ bit) for a in range(count)])
        high = (me & bit) > 0
        first = jnp.where(high, other, value)
        second = jnp.where(high, value, other)
        value = jnp.stack([first, second], axis=1).reshape((-1,) + value.shape[1:])
        bit //= 2
    return value


def local(queries, key_rows, value_rows, pair_keys, pair_values, first_key, residual, out_weight):
    tok = queries.shape[0]
    width = queries.shape[1]
    seq_size, head_size = lax.axis_size("seq"), lax.axis_size("head")
    block = jnp.concatenate(
        [
            jnp.concatenate([key_rows, value_rows], axis=1),
            jnp.concatenate([pair_keys[tok - W2 :], pair_values[tok - W2 :]], axis=1),
        ],
        axis=0,
    )
    context, own = context_blocks(block, (W1 + tok - 1) // tok)
    base = lax.axis_index("seq") * tok
    own, base = (jnp.asarray(value, jnp.int32).reshape(1) for value in (own, base))
    tile = TILE * DH

    def attend(start, count):
        parts = []
        for at in range(0, width, tile):
            q = queries[:, at : at + tile]
            if q.shape[1] < tile:
                q = jnp.pad(q, ((0, 0), (0, tile - q.shape[1])))
            parts.append(
                attention(start, count, own, base, first_key, q, context, pair_keys, pair_values)
            )
        return (parts[0] if len(parts) == 1 else jnp.concatenate(parts, axis=1))[:, :width]

    columns = out_weight.shape[1]
    rows = tok // head_size
    every = gathered(attend(0, tok)).reshape(seq_size * tok, width)
    partial_rows = jnp.dot(every, out_weight, preferred_element_type=jnp.float32)
    sent = partial_rows.astype(jnp.bfloat16).reshape(seq_size * head_size, rows, columns)
    got = lax.all_to_all(sent, ("seq", "head"), 0, 0).reshape(seq_size, head_size, rows, columns)
    summed = jnp.sum(got.astype(jnp.float32), axis=1)
    return residual + jnp.swapaxes(summed, 0, 1).reshape(rows, seq_size * columns)


def solution(mesh):
    placed = (
        P("seq", "head"),
        P("seq", None),
        P("seq", None),
        P("seq", None),
        P("seq", None),
        P("seq"),
        P(("seq", "head"), None),
        P("head", "seq"),
    )
    return jax.shard_map(
        local, mesh=mesh, in_specs=placed, out_specs=P(("seq", "head"), None), check_vma=False
    )
```

```python
import functools
import math

import jax
import jax.numpy as jnp
from jax import lax
from jax.experimental import pallas as pl
from jax.experimental.pallas import tpu as pltpu
from jax.sharding import PartitionSpec as P

DH = 128
W1 = 512
W2 = 32
BLOCK = 128
LOW = -1e30
TILE = 8
GROUP = 4
GROUPS = 2
ROWS = TILE * W2


def attention_kernel(
    token_at, skip, steps, most, tok, own_ref, base_ref, first_ref, q_hbm, ctx_hbm, *rest,
    held,
):
    if held:
        w_hbm, out_ref, w_out, *rest = rest
    else:
        out_ref, *rest = rest
    q_ref, ctx_ref, qf, of, pkf, pk2, pvb, kx, vx, lhs, scores, weights, arrived = rest
    copies = [
        pltpu.make_async_copy(source, target, arrived.at[index])
        for index, (source, target) in enumerate(
            [(ctx_hbm, ctx_ref), (q_hbm, q_ref)]
        )
    ]
    if held:
        weight = pltpu.make_async_copy(w_hbm, w_out, arrived.at[2])
        weight.start()
    for copy in copies:
        copy.start()
    unit = GROUP * ROWS
    row = lax.broadcasted_iota(jnp.int32, (unit, DH), 0)
    col = lax.broadcasted_iota(jnp.int32, (unit, DH), 1)
    pick = jnp.where(row // TILE == col, 1.0, 0.0).astype(jnp.bfloat16)
    for g in range(GROUPS):
        lhs[g * unit : (g + 1) * unit, DH:] = pick
    for copy in copies:
        copy.wait()
    blocks = kx.shape[1] // BLOCK
    own = own_ref[0]
    base = base_ref[0]
    origin = base - own * tok
    for b in range(blocks):
        rows = slice(b * BLOCK, (b + 1) * BLOCK)
        for g in range(GROUPS):
            kx[g, rows, :DH] = ctx_ref[rows, :DH]
        vx[rows, :DH] = ctx_ref[rows, DH : 2 * DH]
        vx[rows, DH:] = jnp.ones((BLOCK, DH), jnp.bfloat16)
    before = pl.multiple_of(jnp.maximum(own * tok - W2, 0), W2)
    pkf[0:W2] = ctx_ref[pl.ds(before, W2), 2 * DH :].astype(jnp.float32)
    pkf[W2 : W2 + tok] = ctx_ref[pl.ds(pl.multiple_of(own * tok, BLOCK), tok), 2 * DH :].astype(jnp.float32)
    pkf[W2 + tok :] = jnp.zeros((8, 2 * DH), jnp.float32)

    def spread(blk, _):
        r0 = pl.multiple_of(blk * 8, 8)
        x = pkf[pl.ds(r0, 16)]
        for r in range(8):
            a = jnp.broadcast_to(x[r : r + 1, :DH], (TILE, DH))
            b = jnp.broadcast_to(x[r + 1 : r + 2, :DH], (TILE, DH))
            pk2[r0 + r] = jnp.concatenate([a, b], axis=0).astype(jnp.bfloat16)
            pvb[r0 + r] = jnp.broadcast_to(x[r : r + 1, DH:], (TILE, DH))
        return 0

    lax.fori_loop(0, (W2 + tok) // 8, spread, 0)
    for h in range(TILE):
        qf[pl.ds(h, tok, stride=TILE), :] = q_ref[:, h * DH : (h + 1) * DH].astype(jnp.float32)
    lane = lax.broadcasted_iota(jnp.int32, (1, DH), 1)
    lane_token = lane // W2
    lane_offset = lane % W2
    factor = math.log2(math.e) / math.sqrt(DH)
    tokens = GROUP * GROUPS

    def step(index, _):
        i0 = token_at + index * skip
        pos0 = base + i0
        first = [first_ref[i0 + t] for t in range(tokens)]
        lowest = jnp.maximum(first[0], pos0 - W1 + 1)
        block_low = (lowest - origin) // BLOCK
        block_high = (pos0 + tokens - 1 - origin) // BLOCK
        start = pl.multiple_of(block_low * BLOCK, BLOCK)

        def run(n):
            keys = n * BLOCK
            key_pos = lax.broadcasted_iota(jnp.int32, (keys, DH), 0) + (origin + start)

            def score(g):
                mine = first[g * GROUP : (g + 1) * GROUP]
                first_lane = jnp.full((1, DH), mine[-1], jnp.int32)
                for t in range(GROUP - 2, -1, -1):
                    first_lane = jnp.where(lane_token == t, mine[t], first_lane)
                high = pos0 + g * GROUP + lane_token
                low = jnp.maximum(first_lane, high - W1 + 1)
                low = jnp.where(high - (W2 - 1) + lane_offset >= first_lane, low, 2**30)
                ok = (key_pos >= low) & (key_pos <= high)
                kx[g, pl.ds(start, keys), DH:] = jnp.where(ok, 0.0, LOW).astype(jnp.bfloat16)
                for t in range(g * GROUP, (g + 1) * GROUP):
                    q = qf[pl.ds(pl.multiple_of((i0 + t) * TILE, TILE), TILE)]
                    q = jnp.concatenate([q, q], axis=0).astype(jnp.bfloat16)
                    for k in range(W2 // 2):
                        at = t * ROWS + k * 16
                        lhs[at : at + 16, :DH] = q * pk2[i0 + t + 1 + 2 * k]
                scores[g * unit : (g + 1) * unit, :keys] = lax.dot_general(
                    lhs[g * unit : (g + 1) * unit],
                    kx[g, pl.ds(start, keys)],
                    (((1,), (1,)), ((), ())),
                    preferred_element_type=jnp.float32,
                )

            def soften(g):
                for t in range(g * GROUP, (g + 1) * GROUP):
                    rows = slice(t * ROWS, (t + 1) * ROWS)
                    s = scores[rows, :keys].reshape(W2, TILE, keys)
                    top = jnp.max(jnp.max(s, axis=0), axis=1, keepdims=True)
                    e = jnp.exp2((s - top[None]) * factor)
                    weights[rows, :keys] = e.reshape(ROWS, keys).astype(jnp.bfloat16)

            def value(g):
                o = jnp.dot(
                    weights[g * unit : (g + 1) * unit, :keys],
                    vx[pl.ds(start, keys)],
                    preferred_element_type=jnp.float32,
                )
                for t in range(GROUP):
                    carried = jnp.zeros((TILE, DH), jnp.float32)
                    total = jnp.zeros((TILE, DH), jnp.float32)
                    for w in range(W2):
                        at = t * ROWS + w * TILE
                        carried += o[at : at + TILE, :DH] * pvb[i0 + g * GROUP + t + 1 + w]
                        total += o[at : at + TILE, DH:]
                    at = pl.multiple_of((index * tokens + g * GROUP + t) * TILE, TILE)
                    of[pl.ds(at, TILE)] = carried / total

            score(0)
            for g in range(GROUPS):
                if g + 1 < GROUPS:
                    score(g + 1)
                soften(g)
                if g >= 1:
                    value(g - 1)
            value(GROUPS - 1)

        for n in range(1, most + 1):
            pl.when(block_high - block_low + 1 == n)(functools.partial(run, n))
        return 0

    lax.fori_loop(0, steps, step, 0)
    count = steps * tokens
    for h in range(TILE):
        out_ref[:, h * DH : (h + 1) * DH] = of[pl.ds(h, count, stride=TILE), :].astype(jnp.bfloat16)
    if held:
        weight.wait()


def attention(token_at, skip, steps, own, base, first_key, q, context, held=None):
    tok = first_key.shape[0]
    count = steps * GROUP * GROUPS
    rows = context.shape[0]
    most = min(rows // BLOCK, W1 // BLOCK + 1)
    f32, bf16 = jnp.float32, jnp.bfloat16
    unit = GROUPS * GROUP * ROWS
    more = [] if held is None else [held]
    out = pl.pallas_call(
        functools.partial(attention_kernel, token_at, skip, steps, most, tok, held=held is not None),
        out_shape=[jax.ShapeDtypeStruct((count, TILE * DH), bf16)]
        + [jax.ShapeDtypeStruct(value.shape, value.dtype) for value in more],
        in_specs=[pl.BlockSpec(memory_space=pltpu.SMEM)] * 3
        + [pl.BlockSpec(memory_space=pl.ANY)] * (2 + len(more)),
        out_specs=[pl.BlockSpec(memory_space=pltpu.VMEM)]
        + [pl.BlockSpec(memory_space=pl.ANY) for value in more],
        scratch_shapes=[
            pltpu.VMEM(q.shape, bf16),
            pltpu.VMEM(context.shape, bf16),
            pltpu.VMEM((tok * TILE, DH), f32),
            pltpu.VMEM((count * TILE, DH), f32),
            pltpu.VMEM((W2 + tok + 8, 2 * DH), f32),
            pltpu.VMEM((W2 + tok, 2 * TILE, DH), bf16),
            pltpu.VMEM((W2 + tok, TILE, DH), f32),
            pltpu.VMEM((GROUPS, rows, 2 * DH), bf16),
            pltpu.VMEM((rows, 2 * DH), bf16),
            pltpu.VMEM((unit, 2 * DH), bf16),
            pltpu.VMEM((unit, most * BLOCK), f32),
            pltpu.VMEM((unit, most * BLOCK), bf16),
            pltpu.SemaphoreType.DMA((3,)),
        ],
        cost_estimate=pl.CostEstimate(
            flops=4 * count * ROWS * most * BLOCK * 2 * DH, bytes_accessed=2**20, transcendentals=0
        ),
        compiler_params=pltpu.CompilerParams(vmem_limit_bytes=24 * 2**20),
        name="attention",
    )(own, base, first_key, q, context, *more)
    return out if more else out[0]


def project_kernel(order, me_ref, kept_ref, came_ref, w_ref, out_ref, rows_ref):
    count = kept_ref.shape[1]
    pieces = [kept_ref[i] for i in range(kept_ref.shape[0])]
    pieces += [came_ref[i] for i in range(came_ref.shape[0])]
    for other, piece in zip(order, pieces, strict=True):
        at = pl.multiple_of((me_ref[0] ^ other) * count, count)
        rows_ref[pl.ds(at, count)] = piece
    columns = w_ref.shape[1]
    width = math.gcd(columns, 512)
    for at in range(0, columns, width):
        out_ref[:, at : at + width] = jnp.dot(
            rows_ref[...], w_ref[:, at : at + width], preferred_element_type=jnp.float32
        ).astype(jnp.bfloat16)


def project(features, out_weight):
    size = lax.axis_size("seq")
    me = lax.axis_index("seq").astype(jnp.int32).reshape(1)
    kept, order, bit = features[None], [0], size // 2
    while bit:
        came = lax.ppermute(kept, "seq", [(a, a ^ bit) for a in range(size)])
        order = order + [other ^ bit for other in order]
        bit //= 2
        if bit:
            kept = jnp.concatenate([kept, came], axis=0)
    rows = size * features.shape[0]
    depth, columns = out_weight.shape
    return pl.pallas_call(
        functools.partial(project_kernel, order),
        out_shape=jax.ShapeDtypeStruct((rows, columns), jnp.bfloat16),
        in_specs=[
            pl.BlockSpec(memory_space=pltpu.SMEM),
            pl.BlockSpec(memory_space=pltpu.VMEM),
            pl.BlockSpec(memory_space=pltpu.VMEM),
            pl.BlockSpec(memory_space=pltpu.VMEM),
        ],
        out_specs=pl.BlockSpec(memory_space=pltpu.VMEM),
        scratch_shapes=[pltpu.VMEM((rows, depth), jnp.bfloat16)],
        cost_estimate=pl.CostEstimate(
            flops=2 * rows * depth * columns, bytes_accessed=2 * depth * columns, transcendentals=0
        ),
        compiler_params=pltpu.CompilerParams(vmem_limit_bytes=20 * 2**20),
        name="project",
    )(me, kept, came, out_weight)


def context_blocks(block, reach):
    count = lax.axis_size("seq")
    if count <= reach + 1:
        return lax.all_gather(block, "seq", axis=0, tiled=True), lax.axis_index("seq")
    pieces = [
        lax.ppermute(block, "seq", [(a, a + steps) for a in range(count - steps)])
        for steps in range(reach, 0, -1)
    ]
    return jnp.concatenate(pieces + [block], axis=0), jnp.int32(reach)


def local(queries, key_rows, value_rows, pair_keys, pair_values, first_key, residual, out_weight):
    tok = queries.shape[0]
    width = queries.shape[1]
    seq_size, head_size = lax.axis_size("seq"), lax.axis_size("head")
    block = jnp.concatenate([key_rows, value_rows, pair_keys, pair_values], axis=1)
    context, own = context_blocks(block, (W1 + tok - 1) // tok)
    base = lax.axis_index("seq") * tok
    own, base = (jnp.asarray(value, jnp.int32).reshape(1) for value in (own, base))
    tile = TILE * DH

    step = GROUP * GROUPS

    def attend(start, skip, steps, queries, held=None):
        parts, copied = [], None
        for at in range(0, width, tile):
            q = queries[:, at : at + tile]
            if q.shape[1] < tile:
                q = jnp.pad(q, ((0, 0), (0, tile - q.shape[1])))
            part = attention(start, skip, steps, own, base, first_key, q, context, held)
            if held is not None:
                part, copied = part
                held = None
            parts.append(part)
        features = (parts[0] if len(parts) == 1 else jnp.concatenate(parts, axis=1))[:, :width]
        return (features, copied) if copied is not None else features

    columns = out_weight.shape[1]
    rows = tok // head_size

    def product(features, count, out_weight):
        return project(features, out_weight).reshape(seq_size * head_size, count, columns)

    def exchange(sent):
        return lax.all_to_all(sent, ("seq", "head"), 0, 0)

    def total(got):
        got = got.reshape(seq_size, head_size, -1, columns).astype(jnp.float32)
        return jnp.swapaxes(jnp.sum(got, axis=1), 0, 1).reshape(-1, seq_size * columns)

    if rows != 2 * step:
        sent = product(attend(0, step, tok // step, queries), rows, out_weight)
        return residual + total(exchange(sent))
    steps = tok // rows
    first = attend(0, rows, steps, queries)
    sent = product(first, step, out_weight)
    queries, sent = lax.optimization_barrier((queries, sent))
    got_first = exchange(sent)
    second = attend(step, rows, steps, queries)
    got_second = exchange(product(second, step, out_weight))
    return residual + jnp.concatenate([total(got_first), total(got_second)], axis=0)


def solution(mesh):
    placed = (
        P("seq", "head"),
        P("seq", None),
        P("seq", None),
        P("seq", None),
        P("seq", None),
        P("seq"),
        P(("seq", "head"), None),
        P("head", "seq"),
    )
    return jax.shard_map(
        local, mesh=mesh, in_specs=placed, out_specs=P(("seq", "head"), None), check_vma=False
    )
```

```python
import functools
import math

import jax
import jax.numpy as jnp
from jax import lax
from jax.experimental import pallas as pl
from jax.experimental.pallas import tpu as pltpu
from jax.sharding import PartitionSpec as P

DH = 128
W1 = 512
W2 = 32
BLOCK = 128
LOW = -1e30
TILE = 8
GROUP = 4
GROUPS = 4
RUN = 2
ROWS = TILE * W2


def attention_kernel(
    token_at, skip, steps, most, tok, own_ref, base_ref, first_ref, q_hbm, ctx_hbm, *rest,
    held,
):
    if held:
        w_hbm, out_ref, w_out, *rest = rest
    else:
        out_ref, *rest = rest
    q_ref, ctx_ref, qf, of, pkf, pk2, pvb, kx, vx, lhs, scores, weights, arrived = rest
    copies = [
        pltpu.make_async_copy(source, target, arrived.at[index])
        for index, (source, target) in enumerate(
            [(ctx_hbm, ctx_ref), (q_hbm, q_ref)]
        )
    ]
    if held:
        weight = pltpu.make_async_copy(w_hbm, w_out, arrived.at[2])
        weight.start()
    for copy in copies:
        copy.start()
    unit = GROUP * ROWS
    row = lax.broadcasted_iota(jnp.int32, (unit, DH), 0)
    col = lax.broadcasted_iota(jnp.int32, (unit, DH), 1)
    pick = jnp.where(row // TILE == col, 1.0, 0.0).astype(jnp.bfloat16)
    for g in range(GROUPS):
        lhs[g * unit : (g + 1) * unit, DH:] = pick
    for copy in copies:
        copy.wait()
    blocks = kx.shape[1] // BLOCK
    own = own_ref[0]
    base = base_ref[0]
    origin = base - own * tok
    for b in range(blocks):
        rows = slice(b * BLOCK, (b + 1) * BLOCK)
        for g in range(GROUPS):
            kx[g, rows, :DH] = ctx_ref[rows, :DH]
        vx[rows, :DH] = ctx_ref[rows, DH : 2 * DH]
        vx[rows, DH:] = jnp.ones((BLOCK, DH), jnp.bfloat16)
    before = pl.multiple_of(jnp.maximum(own * tok - W2, 0), W2)
    pkf[0:W2] = ctx_ref[pl.ds(before, W2), 2 * DH :].astype(jnp.float32)
    pkf[W2 : W2 + tok] = ctx_ref[pl.ds(pl.multiple_of(own * tok, BLOCK), tok), 2 * DH :].astype(jnp.float32)
    pkf[W2 + tok :] = jnp.zeros((8, 2 * DH), jnp.float32)

    def spread(blk, _):
        r0 = pl.multiple_of(blk * 8, 8)
        x = pkf[pl.ds(r0, 16)]
        for r in range(8):
            a = jnp.broadcast_to(x[r : r + 1, :DH], (TILE, DH))
            b = jnp.broadcast_to(x[r + 1 : r + 2, :DH], (TILE, DH))
            pk2[r0 + r] = jnp.concatenate([a, b], axis=0).astype(jnp.bfloat16)
            pvb[r0 + r] = jnp.broadcast_to(x[r : r + 1, DH:], (TILE, DH))
        return 0

    lax.fori_loop(0, (W2 + tok) // 8, spread, 0)
    for h in range(TILE):
        qf[pl.ds(h, tok, stride=TILE), :] = q_ref[:, h * DH : (h + 1) * DH].astype(jnp.float32)
    lane = lax.broadcasted_iota(jnp.int32, (1, DH), 1)
    lane_token = lane // W2
    lane_offset = lane % W2
    factor = math.log2(math.e) / math.sqrt(DH)
    tokens = GROUP * GROUPS

    def step(index, _):
        begin = [
            token_at + (index * (GROUPS // RUN) + g // RUN) * skip + g % RUN * GROUP
            for g in range(GROUPS)
        ]
        pos0 = base + begin[0]
        first = [first_ref[begin[t // GROUP] + t % GROUP] for t in range(tokens)]
        lowest = jnp.maximum(first[0], pos0 - W1 + 1)
        block_low = (lowest - origin) // BLOCK
        block_high = (base + begin[-1] + GROUP - 1 - origin) // BLOCK
        start = pl.multiple_of(block_low * BLOCK, BLOCK)

        def run(n):
            keys = n * BLOCK
            key_pos = lax.broadcasted_iota(jnp.int32, (keys, DH), 0) + (origin + start)

            def score(g):
                mine = first[g * GROUP : (g + 1) * GROUP]
                first_lane = jnp.full((1, DH), mine[-1], jnp.int32)
                for t in range(GROUP - 2, -1, -1):
                    first_lane = jnp.where(lane_token == t, mine[t], first_lane)
                high = base + begin[g] + lane_token
                low = jnp.maximum(first_lane, high - W1 + 1)
                low = jnp.where(high - (W2 - 1) + lane_offset >= first_lane, low, 2**30)
                ok = (key_pos >= low) & (key_pos <= high)
                kx[g, pl.ds(start, keys), DH:] = jnp.where(ok, 0.0, LOW).astype(jnp.bfloat16)
                for t in range(g * GROUP, (g + 1) * GROUP):
                    token = begin[g] + t % GROUP
                    q = qf[pl.ds(pl.multiple_of(token * TILE, TILE), TILE)]
                    q = jnp.concatenate([q, q], axis=0).astype(jnp.bfloat16)
                    for k in range(W2 // 2):
                        at = t * ROWS + k * 16
                        lhs[at : at + 16, :DH] = q * pk2[token + 1 + 2 * k]
                scores[g * unit : (g + 1) * unit, :keys] = lax.dot_general(
                    lhs[g * unit : (g + 1) * unit],
                    kx[g, pl.ds(start, keys)],
                    (((1,), (1,)), ((), ())),
                    preferred_element_type=jnp.float32,
                )

            def soften(g):
                for t in range(g * GROUP, (g + 1) * GROUP):
                    rows = slice(t * ROWS, (t + 1) * ROWS)
                    s = scores[rows, :keys].reshape(W2, TILE, keys)
                    top = jnp.max(jnp.max(s, axis=0), axis=1, keepdims=True)
                    e = jnp.exp2((s - top[None]) * factor)
                    weights[rows, :keys] = e.reshape(ROWS, keys).astype(jnp.bfloat16)

            def value(g):
                o = jnp.dot(
                    weights[g * unit : (g + 1) * unit, :keys],
                    vx[pl.ds(start, keys)],
                    preferred_element_type=jnp.float32,
                )
                for t in range(GROUP):
                    carried = jnp.zeros((TILE, DH), jnp.float32)
                    total = jnp.zeros((TILE, DH), jnp.float32)
                    for w in range(W2):
                        at = t * ROWS + w * TILE
                        carried += o[at : at + TILE, :DH] * pvb[begin[g] + t + 1 + w]
                        total += o[at : at + TILE, DH:]
                    at = pl.multiple_of((index * tokens + g * GROUP + t) * TILE, TILE)
                    of[pl.ds(at, TILE)] = carried / total

            score(0)
            for g in range(GROUPS):
                if g + 1 < GROUPS:
                    score(g + 1)
                soften(g)
                if g >= 1:
                    value(g - 1)
            value(GROUPS - 1)

        for n in range(1, most + 1):
            pl.when(block_high - block_low + 1 == n)(functools.partial(run, n))
        return 0

    count = steps * GROUP * RUN
    lax.fori_loop(0, count // tokens, step, 0)
    for h in range(TILE):
        out_ref[:, h * DH : (h + 1) * DH] = of[pl.ds(h, count, stride=TILE), :].astype(jnp.bfloat16)
    if held:
        weight.wait()


def attention(token_at, skip, steps, own, base, first_key, q, context, held=None):
    tok = first_key.shape[0]
    count = steps * GROUP * RUN
    rows = context.shape[0]
    span = W1 + (GROUPS // RUN - 1) * skip + RUN * GROUP - 1
    most = min(rows // BLOCK, (span + BLOCK - 2) // BLOCK + 1)
    f32, bf16 = jnp.float32, jnp.bfloat16
    unit = GROUPS * GROUP * ROWS
    more = [] if held is None else [held]
    out = pl.pallas_call(
        functools.partial(attention_kernel, token_at, skip, steps, most, tok, held=held is not None),
        out_shape=[jax.ShapeDtypeStruct((count, TILE * DH), bf16)]
        + [jax.ShapeDtypeStruct(value.shape, value.dtype) for value in more],
        in_specs=[pl.BlockSpec(memory_space=pltpu.SMEM)] * 3
        + [pl.BlockSpec(memory_space=pl.ANY)] * (2 + len(more)),
        out_specs=[pl.BlockSpec(memory_space=pltpu.VMEM)]
        + [pl.BlockSpec(memory_space=pl.ANY) for value in more],
        scratch_shapes=[
            pltpu.VMEM(q.shape, bf16),
            pltpu.VMEM(context.shape, bf16),
            pltpu.VMEM((tok * TILE, DH), f32),
            pltpu.VMEM((count * TILE, DH), f32),
            pltpu.VMEM((W2 + tok + 8, 2 * DH), f32),
            pltpu.VMEM((W2 + tok, 2 * TILE, DH), bf16),
            pltpu.VMEM((W2 + tok, TILE, DH), f32),
            pltpu.VMEM((GROUPS, rows, 2 * DH), bf16),
            pltpu.VMEM((rows, 2 * DH), bf16),
            pltpu.VMEM((unit, 2 * DH), bf16),
            pltpu.VMEM((unit, most * BLOCK), f32),
            pltpu.VMEM((unit, most * BLOCK), bf16),
            pltpu.SemaphoreType.DMA((3,)),
        ],
        cost_estimate=pl.CostEstimate(
            flops=4 * count * ROWS * most * BLOCK * 2 * DH, bytes_accessed=2**20, transcendentals=0
        ),
        compiler_params=pltpu.CompilerParams(vmem_limit_bytes=30 * 2**20),
        name="attention",
    )(own, base, first_key, q, context, *more)
    return out if more else out[0]


def project_kernel(order, split, me_ref, *refs):
    if split:
        bits, refs = refs[:2], refs[2:]
    w_ref, *refs = refs
    kept_ref, came_ref, *outs, rows_ref = refs
    count = kept_ref.shape[1]
    pieces = [ref.at[i] for ref in (kept_ref, came_ref) for i in range(ref.shape[0])]
    for other, piece in zip(order, pieces, strict=True):
        at = pl.multiple_of((me_ref[0] ^ other) * count, count)
        rows_ref[pl.ds(at, count)] = piece[...]
    columns = w_ref.shape[1]

    def product(start, width):
        return jnp.dot(
            rows_ref[...], w_ref[:, pl.ds(start, width)], preferred_element_type=jnp.float32
        )

    if not split:
        width = math.gcd(columns, 512)
        for at in range(0, columns, width):
            outs[0][:, at : at + width] = jnp.dot(
                rows_ref[...], w_ref[:, at : at + width], preferred_element_type=jnp.float32
            ).astype(jnp.bfloat16)
        return
    sum_ref, *sent_refs = outs
    quarter = columns // 4
    for index, sent_ref in enumerate(sent_refs):
        mine = bits[index][0]
        start = pl.multiple_of(index * 2 * quarter + (1 - mine) * quarter, 128)
        sent_ref[...] = product(start, quarter).astype(jnp.bfloat16)
    for index in range(len(sent_refs)):
        mine = bits[index][0]
        start = pl.multiple_of(index * 2 * quarter + mine * quarter, 128)
        sum_ref[:, index * quarter : (index + 1) * quarter] = product(start, quarter)


def swapped(value, axis, bit):
    return lax.ppermute(value, axis, [(a, a ^ bit) for a in range(lax.axis_size(axis))])


def project(features, out_weight, split=False):
    size = lax.axis_size("seq")
    head = lax.axis_index("head")
    places = [lax.axis_index("seq")]
    if split:
        places += [head % 2, head // 2 % 2]
    places = [place.astype(jnp.int32).reshape(1) for place in places]
    kept, order, bit = features[None], [0], size // 2
    while bit:
        came = swapped(kept, "seq", bit)
        order = order + [other ^ bit for other in order]
        bit //= 2
        if bit:
            kept = jnp.concatenate([kept, came], axis=0)
    rows = size * features.shape[0]
    depth, columns = out_weight.shape
    shapes = jax.ShapeDtypeStruct((rows, columns), jnp.bfloat16)
    memory = pl.BlockSpec(memory_space=pltpu.VMEM)
    if split:
        shapes = [jax.ShapeDtypeStruct((rows, columns // 2), jnp.float32)]
        shapes += [jax.ShapeDtypeStruct((rows, columns // 4), jnp.bfloat16)] * 2
    return pl.pallas_call(
        functools.partial(project_kernel, order, split),
        out_shape=shapes,
        in_specs=[pl.BlockSpec(memory_space=pltpu.SMEM)] * len(places)
        + [pl.BlockSpec(memory_space=pltpu.VMEM)] * 3,
        out_specs=[memory] * 3 if split else memory,
        scratch_shapes=[pltpu.VMEM((rows, depth), jnp.bfloat16)],
        cost_estimate=pl.CostEstimate(
            flops=2 * rows * depth * columns, bytes_accessed=2 * depth * columns, transcendentals=0
        ),
        compiler_params=pltpu.CompilerParams(vmem_limit_bytes=20 * 2**20),
        name="project",
    )(*places, out_weight, kept, came)


def context_blocks(block, reach):
    count = lax.axis_size("seq")
    if count <= reach + 1:
        return lax.all_gather(block, "seq", axis=0, tiled=True), lax.axis_index("seq")
    pieces = [
        lax.ppermute(block, "seq", [(a, a + steps) for a in range(count - steps)])
        for steps in range(reach, 0, -1)
    ]
    return jnp.concatenate(pieces + [block], axis=0), jnp.int32(reach)


def local(queries, key_rows, value_rows, pair_keys, pair_values, first_key, residual, out_weight):
    tok = queries.shape[0]
    width = queries.shape[1]
    seq_size, head_size = lax.axis_size("seq"), lax.axis_size("head")
    block = jnp.concatenate([key_rows, value_rows, pair_keys, pair_values], axis=1)
    context, own = context_blocks(block, (W1 + tok - 1) // tok)
    base = lax.axis_index("seq") * tok
    own, base = (jnp.asarray(value, jnp.int32).reshape(1) for value in (own, base))
    tile = TILE * DH

    step = GROUP * RUN

    def attend(start, skip, steps, base):
        parts = []
        for at in range(0, width, tile):
            q = queries[:, at : at + tile]
            if q.shape[1] < tile:
                q = jnp.pad(q, ((0, 0), (0, tile - q.shape[1])))
            parts.append(attention(start, skip, steps, own, base, first_key, q, context))
        return (parts[0] if len(parts) == 1 else jnp.concatenate(parts, axis=1))[:, :width]

    columns = out_weight.shape[1]
    rows = tok // head_size

    def product(features, count, split=False):
        rows_out = project(features, out_weight, split)
        return rows_out if split else rows_out.reshape(seq_size * head_size, count, columns)

    def add_pairs(kept, came):
        rows_out = (kept + jnp.concatenate(came, axis=1).astype(jnp.float32)).astype(jnp.bfloat16)
        return rows_out.reshape(seq_size * head_size, -1, columns // 2)

    def exchange(sent):
        return lax.all_to_all(sent, ("seq", "head"), 0, 0)

    def total(got):
        got = got.reshape(seq_size, head_size, -1, columns).astype(jnp.float32)
        return jnp.swapaxes(jnp.sum(got, axis=1), 0, 1).reshape(-1, seq_size * columns)

    def total_split(got):
        quarter = columns // 4
        got = got.reshape(seq_size, head_size // 4, 2, 2, -1, 2, quarter).astype(jnp.float32)
        near = jnp.sum(got[..., 0, :], axis=(1, 2))
        far = jnp.sum(got[..., 1, :], axis=(1, 3))
        both = jnp.stack([near, far], axis=1)
        return jnp.moveaxis(both, 3, 0).reshape(-1, seq_size * columns)

    if rows != 2 * step or head_size % 4:
        sent = product(attend(0, step, tok // step, base), rows)
        return residual + total(exchange(sent))
    steps = tok // rows
    first = attend(0, rows, steps, base)
    sent = product(first, step)
    base, sent = lax.optimization_barrier((base, sent))
    got_first = exchange(sent)
    second = attend(step, rows, steps, base)
    kept, *leaving = product(second, step, True)
    came = [swapped(value, "head", bit) for value, bit in zip(leaving, (1, 2), strict=True)]
    sent, got_first = lax.optimization_barrier((add_pairs(kept, came), got_first))
    got_second = exchange(sent)
    return residual + jnp.concatenate([total(got_first), total_split(got_second)], axis=0)


def solution(mesh):
    placed = (
        P("seq", "head"),
        P("seq", None),
        P("seq", None),
        P("seq", None),
        P("seq", None),
        P("seq"),
        P(("seq", "head"), None),
        P("head", "seq"),
    )
    return jax.shard_map(
        local, mesh=mesh, in_specs=placed, out_specs=P(("seq", "head"), None), check_vma=False
    )
```

```python
import functools
import math

import jax
import jax.numpy as jnp
from jax import lax
from jax.experimental import pallas as pl
from jax.experimental.pallas import tpu as pltpu
from jax.sharding import PartitionSpec as P

DH = 128
W1 = 512
W2 = 32
BLOCK = 128
LOW = -1e30
TILE = 8
GROUP = 4
GROUPS = 4
RUN = 2
ROWS = TILE * W2


def attention_kernel(
    token_at, skip, steps, most, tok, own_ref, base_ref, first_ref, q_hbm, ctx_hbm, *rest,
    held,
):
    if held:
        w_hbm, out_ref, w_out, *rest = rest
    else:
        out_ref, *rest = rest
    q_ref, ctx_ref, qf, of, pkf, pk2, pvb, kx, vx, lhs, scores, weights, arrived = rest
    copies = [
        pltpu.make_async_copy(source, target, arrived.at[index])
        for index, (source, target) in enumerate(
            [(ctx_hbm, ctx_ref), (q_hbm, q_ref)]
        )
    ]
    if held:
        weight = pltpu.make_async_copy(w_hbm, w_out, arrived.at[2])
        weight.start()
    for copy in copies:
        copy.start()
    unit = GROUP * ROWS
    row = lax.broadcasted_iota(jnp.int32, (unit, DH), 0)
    col = lax.broadcasted_iota(jnp.int32, (unit, DH), 1)
    pick = jnp.where(row // TILE == col, 1.0, 0.0).astype(jnp.bfloat16)
    for g in range(GROUPS):
        lhs[g * unit : (g + 1) * unit, DH:] = pick
    for copy in copies:
        copy.wait()
    blocks = kx.shape[1] // BLOCK
    own = own_ref[0]
    base = base_ref[0]
    origin = base - own * tok
    for b in range(blocks):
        rows = slice(b * BLOCK, (b + 1) * BLOCK)
        for g in range(GROUPS):
            kx[g, rows, :DH] = ctx_ref[rows, :DH]
        vx[rows, :DH] = ctx_ref[rows, DH : 2 * DH]
        vx[rows, DH:] = jnp.ones((BLOCK, DH), jnp.bfloat16)
    before = pl.multiple_of(jnp.maximum(own * tok - W2, 0), W2)
    pkf[0:W2] = ctx_ref[pl.ds(before, W2), 2 * DH :].astype(jnp.float32)
    pkf[W2 : W2 + tok] = ctx_ref[pl.ds(pl.multiple_of(own * tok, BLOCK), tok), 2 * DH :].astype(jnp.float32)
    pkf[W2 + tok :] = jnp.zeros((8, 2 * DH), jnp.float32)

    def spread(blk, _):
        r0 = pl.multiple_of(blk * 8, 8)
        x = pkf[pl.ds(r0, 16)]
        for r in range(8):
            a = jnp.broadcast_to(x[r : r + 1, :DH], (TILE, DH))
            b = jnp.broadcast_to(x[r + 1 : r + 2, :DH], (TILE, DH))
            pk2[r0 + r] = jnp.concatenate([a, b], axis=0).astype(jnp.bfloat16)
            pvb[r0 + r] = jnp.broadcast_to(x[r : r + 1, DH:], (TILE, DH))
        return 0

    lax.fori_loop(0, (W2 + tok) // 8, spread, 0)
    for h in range(TILE):
        qf[pl.ds(h, tok, stride=TILE), :] = q_ref[:, h * DH : (h + 1) * DH].astype(jnp.float32)
    lane = lax.broadcasted_iota(jnp.int32, (1, DH), 1)
    lane_token = lane // W2
    lane_offset = lane % W2
    factor = math.log2(math.e) / math.sqrt(DH)
    tokens = GROUP * GROUPS

    def step(index, _):
        begin = [
            token_at + (index * (GROUPS // RUN) + g // RUN) * skip + g % RUN * GROUP
            for g in range(GROUPS)
        ]
        pos0 = base + begin[0]
        first = [first_ref[begin[t // GROUP] + t % GROUP] for t in range(tokens)]
        lowest = jnp.maximum(first[0], pos0 - W1 + 1)
        block_low = (lowest - origin) // BLOCK
        block_high = (base + begin[-1] + GROUP - 1 - origin) // BLOCK
        start = pl.multiple_of(block_low * BLOCK, BLOCK)

        def run(n):
            keys = n * BLOCK
            key_pos = lax.broadcasted_iota(jnp.int32, (keys, DH), 0) + (origin + start)

            def score(g):
                mine = first[g * GROUP : (g + 1) * GROUP]
                first_lane = jnp.full((1, DH), mine[-1], jnp.int32)
                for t in range(GROUP - 2, -1, -1):
                    first_lane = jnp.where(lane_token == t, mine[t], first_lane)
                high = base + begin[g] + lane_token
                low = jnp.maximum(first_lane, high - W1 + 1)
                low = jnp.where(high - (W2 - 1) + lane_offset >= first_lane, low, 2**30)
                ok = (key_pos >= low) & (key_pos <= high)
                kx[g, pl.ds(start, keys), DH:] = jnp.where(ok, 0.0, LOW).astype(jnp.bfloat16)
                for t in range(g * GROUP, (g + 1) * GROUP):
                    token = begin[g] + t % GROUP
                    q = qf[pl.ds(pl.multiple_of(token * TILE, TILE), TILE)]
                    q = jnp.concatenate([q, q], axis=0).astype(jnp.bfloat16)
                    for k in range(W2 // 2):
                        at = t * ROWS + k * 16
                        lhs[at : at + 16, :DH] = q * pk2[token + 1 + 2 * k]
                scores[g * unit : (g + 1) * unit, :keys] = lax.dot_general(
                    lhs[g * unit : (g + 1) * unit],
                    kx[g, pl.ds(start, keys)],
                    (((1,), (1,)), ((), ())),
                    preferred_element_type=jnp.float32,
                )

            def soften(g):
                for t in range(g * GROUP, (g + 1) * GROUP):
                    rows = slice(t * ROWS, (t + 1) * ROWS)
                    s = scores[rows, :keys].reshape(W2, TILE, keys)
                    top = jnp.max(jnp.max(s, axis=0), axis=1, keepdims=True)
                    e = jnp.exp2((s - top[None]) * factor)
                    weights[rows, :keys] = e.reshape(ROWS, keys).astype(jnp.bfloat16)

            def value(g):
                o = jnp.dot(
                    weights[g * unit : (g + 1) * unit, :keys],
                    vx[pl.ds(start, keys)],
                    preferred_element_type=jnp.float32,
                )
                for t in range(GROUP):
                    carried = jnp.zeros((TILE, DH), jnp.float32)
                    total = jnp.zeros((TILE, DH), jnp.float32)
                    for w in range(W2):
                        at = t * ROWS + w * TILE
                        carried += o[at : at + TILE, :DH] * pvb[begin[g] + t + 1 + w]
                        total += o[at : at + TILE, DH:]
                    at = pl.multiple_of((index * tokens + g * GROUP + t) * TILE, TILE)
                    of[pl.ds(at, TILE)] = carried / total

            score(0)
            for g in range(GROUPS):
                if g + 1 < GROUPS:
                    score(g + 1)
                soften(g)
                if g >= 1:
                    value(g - 1)
            value(GROUPS - 1)

        for n in range(1, most + 1):
            pl.when(block_high - block_low + 1 == n)(functools.partial(run, n))
        return 0

    count = steps * GROUP * RUN
    lax.fori_loop(0, count // tokens, step, 0)
    for h in range(TILE):
        out_ref[:, h * DH : (h + 1) * DH] = of[pl.ds(h, count, stride=TILE), :].astype(jnp.bfloat16)
    if held:
        weight.wait()


def attention(token_at, skip, steps, own, base, first_key, q, context, held=None):
    tok = first_key.shape[0]
    count = steps * GROUP * RUN
    rows = context.shape[0]
    span = W1 + (GROUPS // RUN - 1) * skip + RUN * GROUP - 1
    most = min(rows // BLOCK, (span + BLOCK - 2) // BLOCK + 1)
    f32, bf16 = jnp.float32, jnp.bfloat16
    unit = GROUPS * GROUP * ROWS
    more = [] if held is None else [held]
    out = pl.pallas_call(
        functools.partial(attention_kernel, token_at, skip, steps, most, tok, held=held is not None),
        out_shape=[jax.ShapeDtypeStruct((count, TILE * DH), bf16)]
        + [jax.ShapeDtypeStruct(value.shape, value.dtype) for value in more],
        in_specs=[pl.BlockSpec(memory_space=pltpu.SMEM)] * 3
        + [pl.BlockSpec(memory_space=pl.ANY)] * (2 + len(more)),
        out_specs=[pl.BlockSpec(memory_space=pltpu.VMEM)]
        + [pl.BlockSpec(memory_space=pl.ANY) for value in more],
        scratch_shapes=[
            pltpu.VMEM(q.shape, bf16),
            pltpu.VMEM(context.shape, bf16),
            pltpu.VMEM((tok * TILE, DH), f32),
            pltpu.VMEM((count * TILE, DH), f32),
            pltpu.VMEM((W2 + tok + 8, 2 * DH), f32),
            pltpu.VMEM((W2 + tok, 2 * TILE, DH), bf16),
            pltpu.VMEM((W2 + tok, TILE, DH), f32),
            pltpu.VMEM((GROUPS, rows, 2 * DH), bf16),
            pltpu.VMEM((rows, 2 * DH), bf16),
            pltpu.VMEM((unit, 2 * DH), bf16),
            pltpu.VMEM((unit, most * BLOCK), f32),
            pltpu.VMEM((unit, most * BLOCK), bf16),
            pltpu.SemaphoreType.DMA((3,)),
        ],
        cost_estimate=pl.CostEstimate(
            flops=4 * count * ROWS * most * BLOCK * 2 * DH, bytes_accessed=2**20, transcendentals=0
        ),
        compiler_params=pltpu.CompilerParams(vmem_limit_bytes=30 * 2**20),
        name="attention",
    )(own, base, first_key, q, context, *more)
    return out if more else out[0]


def project_kernel(order, split, w_ref, *refs):
    me, head = lax.axis_index("seq"), lax.axis_index("head")
    bits = [head % 2, head // 2 % 2]
    kept_ref, came_ref, *outs, rows_ref = refs
    count = kept_ref.shape[1]
    pieces = [ref.at[i] for ref in (kept_ref, came_ref) for i in range(ref.shape[0])]
    for other, piece in zip(order, pieces, strict=True):
        at = pl.multiple_of((me ^ other) * count, count)
        rows_ref[pl.ds(at, count)] = piece[...]
    columns = w_ref.shape[1]

    def product(start, width):
        return jnp.dot(
            rows_ref[...], w_ref[:, pl.ds(start, width)], preferred_element_type=jnp.float32
        )

    if not split:
        width = math.gcd(columns, 512)
        for at in range(0, columns, width):
            outs[0][:, at : at + width] = jnp.dot(
                rows_ref[...], w_ref[:, at : at + width], preferred_element_type=jnp.float32
            ).astype(jnp.bfloat16)
        return
    sum_ref, *sent_refs = outs
    quarter = columns // 4
    for index, sent_ref in enumerate(sent_refs):
        mine = bits[index]
        start = pl.multiple_of(index * 2 * quarter + (1 - mine) * quarter, 128)
        sent_ref[...] = product(start, quarter).astype(jnp.bfloat16)
    for index in range(len(sent_refs)):
        mine = bits[index]
        start = pl.multiple_of(index * 2 * quarter + mine * quarter, 128)
        sum_ref[:, index * quarter : (index + 1) * quarter] = product(start, quarter)


def swapped(value, axis, bit):
    return lax.ppermute(value, axis, [(a, a ^ bit) for a in range(lax.axis_size(axis))])


def project(features, out_weight, split=False):
    size = lax.axis_size("seq")
    kept, order, bit = features[None], [0], size // 2
    while bit:
        came = swapped(kept, "seq", bit)
        order = order + [other ^ bit for other in order]
        bit //= 2
        if bit:
            kept = jnp.concatenate([kept, came], axis=0)
    rows = size * features.shape[0]
    depth, columns = out_weight.shape
    shapes = jax.ShapeDtypeStruct((rows, columns), jnp.bfloat16)
    memory = pl.BlockSpec(memory_space=pltpu.VMEM)
    if split:
        shapes = [jax.ShapeDtypeStruct((rows, columns // 2), jnp.float32)]
        shapes += [jax.ShapeDtypeStruct((rows, columns // 4), jnp.bfloat16)] * 2
    return pl.pallas_call(
        functools.partial(project_kernel, order, split),
        out_shape=shapes,
        in_specs=[pl.BlockSpec(memory_space=pltpu.VMEM)] * 3,
        out_specs=[memory] * 3 if split else memory,
        scratch_shapes=[pltpu.VMEM((rows, depth), jnp.bfloat16)],
        cost_estimate=pl.CostEstimate(
            flops=2 * rows * depth * columns, bytes_accessed=2 * depth * columns, transcendentals=0
        ),
        compiler_params=pltpu.CompilerParams(vmem_limit_bytes=20 * 2**20),
        name="project",
    )(out_weight, kept, came)


def context_blocks(block, reach):
    count = lax.axis_size("seq")
    if count <= reach + 1:
        return lax.all_gather(block, "seq", axis=0, tiled=True), lax.axis_index("seq")
    pieces = [
        lax.ppermute(block, "seq", [(a, a + steps) for a in range(count - steps)])
        for steps in range(reach, 0, -1)
    ]
    return jnp.concatenate(pieces + [block], axis=0), jnp.int32(reach)


def local(queries, key_rows, value_rows, pair_keys, pair_values, first_key, residual, out_weight):
    tok = queries.shape[0]
    width = queries.shape[1]
    seq_size, head_size = lax.axis_size("seq"), lax.axis_size("head")
    block = jnp.concatenate([key_rows, value_rows, pair_keys, pair_values], axis=1)
    context, own = context_blocks(block, (W1 + tok - 1) // tok)
    base = lax.axis_index("seq") * tok
    own, base = (jnp.asarray(value, jnp.int32).reshape(1) for value in (own, base))
    tile = TILE * DH

    step = GROUP * RUN

    def attend(start, skip, steps, base):
        parts = []
        for at in range(0, width, tile):
            q = queries[:, at : at + tile]
            if q.shape[1] < tile:
                q = jnp.pad(q, ((0, 0), (0, tile - q.shape[1])))
            parts.append(attention(start, skip, steps, own, base, first_key, q, context))
        return (parts[0] if len(parts) == 1 else jnp.concatenate(parts, axis=1))[:, :width]

    columns = out_weight.shape[1]
    rows = tok // head_size

    def product(features, count, split=False):
        rows_out = project(features, out_weight, split)
        return rows_out if split else rows_out.reshape(seq_size * head_size, count, columns)

    def add_pairs(kept, came):
        rows_out = (kept + jnp.concatenate(came, axis=1).astype(jnp.float32)).astype(jnp.bfloat16)
        return rows_out.reshape(seq_size * head_size, -1, columns // 2)

    def exchange(sent):
        return lax.all_to_all(sent, ("seq", "head"), 0, 0)

    def total(got):
        got = got.reshape(seq_size, head_size, -1, columns).astype(jnp.float32)
        return jnp.swapaxes(jnp.sum(got, axis=1), 0, 1).reshape(-1, seq_size * columns)

    def total_split(got):
        quarter = columns // 4
        got = got.reshape(seq_size, head_size // 4, 2, 2, -1, 2, quarter).astype(jnp.float32)
        near = jnp.sum(got[..., 0, :], axis=(1, 2))
        far = jnp.sum(got[..., 1, :], axis=(1, 3))
        both = jnp.stack([near, far], axis=1)
        return jnp.moveaxis(both, 3, 0).reshape(-1, seq_size * columns)

    if rows != 2 * step or head_size % 4:
        sent = product(attend(0, step, tok // step, base), rows)
        return residual + total(exchange(sent))
    steps = tok // rows
    first = attend(0, rows, steps, base)
    sent = product(first, step)
    base, sent = lax.optimization_barrier((base, sent))
    got_first = exchange(sent)
    second = attend(step, rows, steps, base)
    kept, *leaving = product(second, step, True)
    came = [swapped(value, "head", bit) for value, bit in zip(leaving, (1, 2), strict=True)]
    sent, got_first = lax.optimization_barrier((add_pairs(kept, came), got_first))
    got_second = exchange(sent)
    return residual + jnp.concatenate([total(got_first), total_split(got_second)], axis=0)


def solution(mesh):
    placed = (
        P("seq", "head"),
        P("seq", None),
        P("seq", None),
        P("seq", None),
        P("seq", None),
        P("seq"),
        P(("seq", "head"), None),
        P("head", "seq"),
    )
    return jax.shard_map(
        local, mesh=mesh, in_specs=placed, out_specs=P(("seq", "head"), None), check_vma=False
    )
```

```python
import functools
import math

import jax
import jax.numpy as jnp
from jax import lax
from jax.experimental import pallas as pl
from jax.experimental.pallas import tpu as pltpu
from jax.sharding import PartitionSpec as P

DH = 128
W1 = 512
W2 = 32
BLOCK = 128
LOW = -1e30
TILE = 8
GROUP = 4
GROUPS = 4
RUN = 2
ROWS = TILE * W2


def attention_kernel(
    token_at, skip, steps, most, tok, ahead, first_ref, q_hbm, ctx_hbm, *rest,
    held,
):
    if held:
        w_hbm, out_ref, w_out, *rest = rest
    else:
        out_ref, *rest = rest
    q_ref, ctx_ref, qf, of, pkf, pk2, pvb, kx, vx, lhs, scores, weights, arrived = rest
    copies = [
        pltpu.make_async_copy(source, target, arrived.at[index])
        for index, (source, target) in enumerate(
            [(ctx_hbm, ctx_ref), (q_hbm, q_ref)]
        )
    ]
    if held:
        weight = pltpu.make_async_copy(w_hbm, w_out, arrived.at[2])
        weight.start()
    for copy in copies:
        copy.start()
    unit = GROUP * ROWS
    row = lax.broadcasted_iota(jnp.int32, (unit, DH), 0)
    col = lax.broadcasted_iota(jnp.int32, (unit, DH), 1)
    pick = jnp.where(row // TILE == col, 1.0, 0.0).astype(jnp.bfloat16)
    for g in range(GROUPS):
        lhs[g * unit : (g + 1) * unit, DH:] = pick
    for copy in copies:
        copy.wait()
    blocks = kx.shape[1] // BLOCK
    place = lax.axis_index("seq")
    own = place if ahead is None else ahead
    base = place * tok
    origin = base - own * tok
    for b in range(blocks):
        rows = slice(b * BLOCK, (b + 1) * BLOCK)
        for g in range(GROUPS):
            kx[g, rows, :DH] = ctx_ref[rows, :DH]
        vx[rows, :DH] = ctx_ref[rows, DH : 2 * DH]
        vx[rows, DH:] = jnp.ones((BLOCK, DH), jnp.bfloat16)
    before = pl.multiple_of(jnp.maximum(own * tok - W2, 0), W2)
    pkf[0:W2] = ctx_ref[pl.ds(before, W2), 2 * DH :].astype(jnp.float32)
    pkf[W2 : W2 + tok] = ctx_ref[pl.ds(pl.multiple_of(own * tok, BLOCK), tok), 2 * DH :].astype(jnp.float32)
    pkf[W2 + tok :] = jnp.zeros((8, 2 * DH), jnp.float32)

    def spread(blk, _):
        r0 = pl.multiple_of(blk * 8, 8)
        x = pkf[pl.ds(r0, 16)]
        for r in range(8):
            a = jnp.broadcast_to(x[r : r + 1, :DH], (TILE, DH))
            b = jnp.broadcast_to(x[r + 1 : r + 2, :DH], (TILE, DH))
            pk2[r0 + r] = jnp.concatenate([a, b], axis=0).astype(jnp.bfloat16)
            pvb[r0 + r] = jnp.broadcast_to(x[r : r + 1, DH:], (TILE, DH))
        return 0

    lax.fori_loop(0, (W2 + tok) // 8, spread, 0)
    for h in range(TILE):
        qf[pl.ds(h, tok, stride=TILE), :] = q_ref[:, h * DH : (h + 1) * DH].astype(jnp.float32)
    lane = lax.broadcasted_iota(jnp.int32, (1, DH), 1)
    lane_token = lane // W2
    lane_offset = lane % W2
    factor = math.log2(math.e) / math.sqrt(DH)
    tokens = GROUP * GROUPS

    def step(index, _):
        begin = [
            token_at + (index * (GROUPS // RUN) + g // RUN) * skip + g % RUN * GROUP
            for g in range(GROUPS)
        ]
        pos0 = base + begin[0]
        first = [first_ref[begin[t // GROUP] + t % GROUP] for t in range(tokens)]
        lowest = jnp.maximum(first[0], pos0 - W1 + 1)
        block_low = (lowest - origin) // BLOCK
        block_high = (base + begin[-1] + GROUP - 1 - origin) // BLOCK
        start = pl.multiple_of(block_low * BLOCK, BLOCK)

        def run(n):
            keys = n * BLOCK
            key_pos = lax.broadcasted_iota(jnp.int32, (keys, DH), 0) + (origin + start)

            def score(g):
                mine = first[g * GROUP : (g + 1) * GROUP]
                first_lane = jnp.full((1, DH), mine[-1], jnp.int32)
                for t in range(GROUP - 2, -1, -1):
                    first_lane = jnp.where(lane_token == t, mine[t], first_lane)
                high = base + begin[g] + lane_token
                low = jnp.maximum(first_lane, high - W1 + 1)
                low = jnp.where(high - (W2 - 1) + lane_offset >= first_lane, low, 2**30)
                ok = (key_pos >= low) & (key_pos <= high)
                kx[g, pl.ds(start, keys), DH:] = jnp.where(ok, 0.0, LOW).astype(jnp.bfloat16)
                for t in range(g * GROUP, (g + 1) * GROUP):
                    token = begin[g] + t % GROUP
                    q = qf[pl.ds(pl.multiple_of(token * TILE, TILE), TILE)]
                    q = jnp.concatenate([q, q], axis=0).astype(jnp.bfloat16)
                    for k in range(W2 // 2):
                        at = t * ROWS + k * 16
                        lhs[at : at + 16, :DH] = q * pk2[token + 1 + 2 * k]
                scores[g * unit : (g + 1) * unit, :keys] = lax.dot_general(
                    lhs[g * unit : (g + 1) * unit],
                    kx[g, pl.ds(start, keys)],
                    (((1,), (1,)), ((), ())),
                    preferred_element_type=jnp.float32,
                )

            def soften(g):
                for t in range(g * GROUP, (g + 1) * GROUP):
                    rows = slice(t * ROWS, (t + 1) * ROWS)
                    s = scores[rows, :keys].reshape(W2, TILE, keys)
                    top = jnp.max(jnp.max(s, axis=0), axis=1, keepdims=True)
                    e = jnp.exp2((s - top[None]) * factor)
                    weights[rows, :keys] = e.reshape(ROWS, keys).astype(jnp.bfloat16)

            def value(g):
                o = jnp.dot(
                    weights[g * unit : (g + 1) * unit, :keys],
                    vx[pl.ds(start, keys)],
                    preferred_element_type=jnp.float32,
                )
                for t in range(GROUP):
                    carried = jnp.zeros((TILE, DH), jnp.float32)
                    total = jnp.zeros((TILE, DH), jnp.float32)
                    for w in range(W2):
                        at = t * ROWS + w * TILE
                        carried += o[at : at + TILE, :DH] * pvb[begin[g] + t + 1 + w]
                        total += o[at : at + TILE, DH:]
                    at = pl.multiple_of((index * tokens + g * GROUP + t) * TILE, TILE)
                    of[pl.ds(at, TILE)] = carried / total

            score(0)
            for g in range(GROUPS):
                if g + 1 < GROUPS:
                    score(g + 1)
                soften(g)
                if g >= 1:
                    value(g - 1)
            value(GROUPS - 1)

        for n in range(1, most + 1):
            pl.when(block_high - block_low + 1 == n)(functools.partial(run, n))
        return 0

    count = steps * GROUP * RUN
    lax.fori_loop(0, count // tokens, step, 0)
    for h in range(TILE):
        out_ref[:, h * DH : (h + 1) * DH] = of[pl.ds(h, count, stride=TILE), :].astype(jnp.bfloat16)
    if held:
        weight.wait()


def attention(token_at, skip, steps, ahead, first_key, q, context, held=None):
    tok = first_key.shape[0]
    count = steps * GROUP * RUN
    rows = context.shape[0]
    span = W1 + (GROUPS // RUN - 1) * skip + RUN * GROUP - 1
    most = min(rows // BLOCK, (span + BLOCK - 2) // BLOCK + 1)
    f32, bf16 = jnp.float32, jnp.bfloat16
    unit = GROUPS * GROUP * ROWS
    more = [] if held is None else [held]
    out = pl.pallas_call(
        functools.partial(
            attention_kernel, token_at, skip, steps, most, tok, ahead, held=held is not None
        ),
        out_shape=[jax.ShapeDtypeStruct((count, TILE * DH), bf16)]
        + [jax.ShapeDtypeStruct(value.shape, value.dtype) for value in more],
        in_specs=[pl.BlockSpec(memory_space=pltpu.SMEM)]
        + [pl.BlockSpec(memory_space=pl.ANY)] * (2 + len(more)),
        out_specs=[pl.BlockSpec(memory_space=pltpu.VMEM)]
        + [pl.BlockSpec(memory_space=pl.ANY) for value in more],
        scratch_shapes=[
            pltpu.VMEM(q.shape, bf16),
            pltpu.VMEM(context.shape, bf16),
            pltpu.VMEM((tok * TILE, DH), f32),
            pltpu.VMEM((count * TILE, DH), f32),
            pltpu.VMEM((W2 + tok + 8, 2 * DH), f32),
            pltpu.VMEM((W2 + tok, 2 * TILE, DH), bf16),
            pltpu.VMEM((W2 + tok, TILE, DH), f32),
            pltpu.VMEM((GROUPS, rows, 2 * DH), bf16),
            pltpu.VMEM((rows, 2 * DH), bf16),
            pltpu.VMEM((unit, 2 * DH), bf16),
            pltpu.VMEM((unit, most * BLOCK), f32),
            pltpu.VMEM((unit, most * BLOCK), bf16),
            pltpu.SemaphoreType.DMA((3,)),
        ],
        cost_estimate=pl.CostEstimate(
            flops=4 * count * ROWS * most * BLOCK * 2 * DH, bytes_accessed=2**20, transcendentals=0
        ),
        compiler_params=pltpu.CompilerParams(vmem_limit_bytes=30 * 2**20),
        name="attention",
    )(first_key, q, context, *more)
    return out if more else out[0]


def project_kernel(order, split, w_ref, *refs):
    me, head = lax.axis_index("seq"), lax.axis_index("head")
    bits = [head % 2, head // 2 % 2]
    pieces, outs, rows_ref = refs[: len(order)], refs[len(order) : -1], refs[-1]
    count = pieces[0].shape[0]
    for other, piece in zip(order, pieces, strict=True):
        at = pl.multiple_of((me ^ other) * count, count)
        rows_ref[pl.ds(at, count)] = piece[...]
    columns = w_ref.shape[1]

    def product(start, width):
        return jnp.dot(
            rows_ref[...], w_ref[:, pl.ds(start, width)], preferred_element_type=jnp.float32
        )

    if not split:
        width = math.gcd(columns, 512)
        for at in range(0, columns, width):
            outs[0][:, at : at + width] = jnp.dot(
                rows_ref[...], w_ref[:, at : at + width], preferred_element_type=jnp.float32
            ).astype(jnp.bfloat16)
        return
    sum_ref, *sent_refs = outs
    quarter = columns // 4
    for index, sent_ref in enumerate(sent_refs):
        mine = bits[index]
        start = pl.multiple_of(index * 2 * quarter + (1 - mine) * quarter, 128)
        sent_ref[...] = product(start, quarter).astype(jnp.bfloat16)
    for index in range(len(sent_refs)):
        mine = bits[index]
        start = pl.multiple_of(index * 2 * quarter + mine * quarter, 128)
        sum_ref[:, index * quarter : (index + 1) * quarter] = product(start, quarter)


def swapped(value, axis, bit):
    return lax.ppermute(value, axis, [(a, a ^ bit) for a in range(lax.axis_size(axis))])


def project(features, out_weight, split=False):
    size = lax.axis_size("seq")
    pieces, bit = {0: features}, size // 2
    while bit:
        for other, piece in list(pieces.items()):
            pieces[other ^ bit] = swapped(piece, "seq", bit)
        bit //= 2
    rows = size * features.shape[0]
    depth, columns = out_weight.shape
    shapes = jax.ShapeDtypeStruct((rows, columns), jnp.bfloat16)
    memory = pl.BlockSpec(memory_space=pltpu.VMEM)
    if split:
        shapes = [jax.ShapeDtypeStruct((rows, columns // 2), jnp.float32)]
        shapes += [jax.ShapeDtypeStruct((rows, columns // 4), jnp.bfloat16)] * 2
    return pl.pallas_call(
        functools.partial(project_kernel, list(pieces), split),
        out_shape=shapes,
        in_specs=[pl.BlockSpec(memory_space=pltpu.VMEM)] * (1 + len(pieces)),
        out_specs=[memory] * 3 if split else memory,
        scratch_shapes=[pltpu.VMEM((rows, depth), jnp.bfloat16)],
        cost_estimate=pl.CostEstimate(
            flops=2 * rows * depth * columns, bytes_accessed=2 * depth * columns, transcendentals=0
        ),
        compiler_params=pltpu.CompilerParams(vmem_limit_bytes=20 * 2**20),
        name="project",
    )(out_weight, *pieces.values())


def context_blocks(block, reach):
    count = lax.axis_size("seq")
    if count <= reach + 1:
        return lax.all_gather(block, "seq", axis=0, tiled=True), None
    pieces = [
        lax.ppermute(block, "seq", [(a, a + steps) for a in range(count - steps)])
        for steps in range(reach, 0, -1)
    ]
    return jnp.concatenate(pieces + [block], axis=0), reach


def local(queries, key_rows, value_rows, pair_keys, pair_values, first_key, residual, out_weight):
    tok = queries.shape[0]
    width = queries.shape[1]
    seq_size, head_size = lax.axis_size("seq"), lax.axis_size("head")
    block = jnp.concatenate([key_rows, value_rows, pair_keys, pair_values], axis=1)
    context, ahead = context_blocks(block, (W1 + tok - 1) // tok)
    tile = TILE * DH

    step = GROUP * RUN

    def attend(start, skip, steps, context):
        parts = []
        for at in range(0, width, tile):
            q = queries[:, at : at + tile]
            if q.shape[1] < tile:
                q = jnp.pad(q, ((0, 0), (0, tile - q.shape[1])))
            parts.append(attention(start, skip, steps, ahead, first_key, q, context))
        return (parts[0] if len(parts) == 1 else jnp.concatenate(parts, axis=1))[:, :width]

    columns = out_weight.shape[1]
    rows = tok // head_size

    def product(features, count, split=False):
        rows_out = project(features, out_weight, split)
        return rows_out if split else rows_out.reshape(seq_size * head_size, count, columns)

    def add_pairs(kept, came):
        rows_out = (kept + jnp.concatenate(came, axis=1).astype(jnp.float32)).astype(jnp.bfloat16)
        return rows_out.reshape(seq_size * head_size, -1, columns // 2)

    def exchange(sent):
        return lax.all_to_all(sent, ("seq", "head"), 0, 0)

    def total(got):
        got = got.reshape(seq_size, head_size, -1, columns).astype(jnp.float32)
        return jnp.swapaxes(jnp.sum(got, axis=1), 0, 1).reshape(-1, seq_size * columns)

    def total_split(got):
        quarter = columns // 4
        got = got.reshape(seq_size, head_size // 4, 2, 2, -1, 2, quarter).astype(jnp.float32)
        near = jnp.sum(got[..., 0, :], axis=(1, 2))
        far = jnp.sum(got[..., 1, :], axis=(1, 3))
        both = jnp.stack([near, far], axis=1)
        return jnp.moveaxis(both, 3, 0).reshape(-1, seq_size * columns)

    if rows != 2 * step or head_size % 4:
        sent = product(attend(0, step, tok // step, context), rows)
        return residual + total(exchange(sent))
    steps = tok // rows
    first = attend(0, rows, steps, context)
    sent = product(first, step)
    context, sent = lax.optimization_barrier((context, sent))
    got_first = exchange(sent)
    second = attend(step, rows, steps, context)
    kept, *leaving = product(second, step, True)
    came = [swapped(value, "head", bit) for value, bit in zip(leaving, (1, 2), strict=True)]
    sent, got_first = lax.optimization_barrier((add_pairs(kept, came), got_first))
    got_second = exchange(sent)
    return residual + jnp.concatenate([total(got_first), total_split(got_second)], axis=0)


def solution(mesh):
    placed = (
        P("seq", "head"),
        P("seq", None),
        P("seq", None),
        P("seq", None),
        P("seq", None),
        P("seq"),
        P(("seq", "head"), None),
        P("head", "seq"),
    )
    return jax.shard_map(
        local, mesh=mesh, in_specs=placed, out_specs=P(("seq", "head"), None), check_vma=False
    )
```
